32 devices in a mesh: kr: 16 (over z, y, x), kc: 2 (over core).
Axes of the slice: x: 2, y: 2, z: 4, core: 2. Of those that a mesh axis runs over, the one named last changes fastest.
Arguments:
- pair_conduction: bfloat16 [384, 64, 4096], P('kr', None, 'kc'), may hold values from -6 to 6
- pair_valence: bfloat16 [384, 64, 4096], P('kr', None, 'kc'), may hold values from -6 to 6
- screened: bfloat16 [16, 4096, 4096], P('kr', 'kc'), may hold values from -0.09375 to 0.09375
- sphere_sizes: int32 [16], replicated, may hold values from 2048 to 4096, as said below
Outputs:
- kernels: float32 [384, 64, 64], P('kr', 'kc')
The draws below stay inside these ranges and needn't reach their ends.
Inputs may be any that keep to these rules, and one draw needn't show every extreme that they name: `sphere_sizes`: each q point's sphere holds 2048 to 4096 G-vectors, and some q point holds all 4096.
All inputs are finite; a program needn't handle non-finite values.
Results may differ from the reference program's by a relative error of at most 0.0029.
Values may be sent and summed in bfloat16 or wider, within the bound.
A program may use at most 128 MiB of HBM per device.

```python
import jax
import jax.numpy as jnp
from jax import lax

G = 4096
NV = 8
NC = 8
PG = 8
NQ = 16
NP = 384


def draw_sphere_sizes(key, part):
    first_key, second_key = jax.random.split(jax.random.fold_in(key, 17))
    sampled = jax.random.randint(first_key, (NQ,), G // 2, G + 1)
    chosen = jax.random.randint(second_key, (), 0, NQ)
    return jnp.where(jnp.arange(NQ) == chosen, G, sampled).astype(jnp.int32)


def shard_levels(key, shape, cuts, low, largest):
    def one(axis_at, parts):
        draws = jax.random.uniform(jax.random.fold_in(jax.random.fold_in(key, 6), axis_at), (parts,), jnp.float32, low / len(cuts), largest / len(cuts))
        return jnp.repeat(jnp.exp(draws), shape[axis_at] // parts).reshape((-1,) + (1,) * (len(shape) - axis_at - 1))

    loudness = one(*cuts[0])
    for cut in cuts[1:]:
        loudness = loudness * one(*cut)
    return loudness


def gaussian(rng, dims, deviation, limit, cuts=(), kind=jnp.bfloat16):
    result = deviation * jax.random.normal(rng, dims, jnp.float32)
    if cuts:
        result = result * shard_levels(rng, dims, cuts, -0.22, 0.18)
    return jnp.clip(result, -limit, limit).astype(kind)


def setup_inputs(seed: int = 0) -> dict:
    splits = jax.random.split(jax.random.key(seed), 5)
    return {
        "pair_conduction": gaussian(splits[0], (NP, NC * NC, G), 1.0, 6.0, ((0, 16), (2, 2))),
        "pair_valence": gaussian(splits[1], (NP, NV * NV, G), 1.0, 6.0, ((0, 16), (2, 2))),
        "screened": gaussian(splits[2], (NQ, G, G), G ** -0.5, 0.09375, ((0, 16), (1, 2))),
        "sphere_sizes": draw_sphere_sizes(jax.random.fold_in(splits[4], 71), 0),
    }


prefactor = 0.015625


def restrict(screen_q, sphere):
    gvector_ids = jnp.arange(G, dtype=jnp.int32)
    inside = gvector_ids < sphere
    keep = inside[:, None] & inside[None, :]
    return jnp.where(keep, screen_q, jnp.zeros((), screen_q.dtype))


def reference(pair_conduction, pair_valence, screened, sphere_sizes):
    conduction = pair_conduction.reshape(NQ, 3, PG, NC * NC, G)
    valence = pair_valence.reshape(NQ, 3, PG, NV * NV, G)

    def one_owner(owner_index):
        results = []
        for group_index, offset in ((0, 0), (1, -1), (2, 1)):
            q_index = (owner_index + offset) % NQ
            screen_q = restrict(screened[q_index], sphere_sizes[q_index])
            applied = jnp.einsum('pbh,gh->pbg', valence[owner_index, group_index].astype(jnp.float32),
                                 screen_q.astype(jnp.float32)).astype(jnp.bfloat16)
            kern_block = jnp.einsum('pag,pbg->pab', conduction[owner_index, group_index].astype(jnp.float32),
                                    applied.astype(jnp.float32))
            results.append(kern_block * prefactor)
        return jnp.stack(results)

    stacked = lax.map(one_owner, jnp.arange(NQ, dtype=jnp.int32))
    return stacked.reshape(NP, NC * NC, NV * NV)
```

```python
import functools

import jax
import jax.numpy as jnp
from jax import lax
from jax.experimental import pallas as pl
from jax.experimental.pallas import tpu as pltpu
from jax.sharding import PartitionSpec as P

prefactor = 0.015625
over_last = (((1,), (1,)), ((), ()))


def at(index, size):
    return pl.ds(pl.multiple_of(index * size, size), size)


def kernel(
    owners, shares, cuts, bands,
    sizes, conduction_hbm, valence_hbm, screened_hbm, out,
    screened, conduction, valence, applied, returned, partial, others,
    load_sem, go_send, go_recv, share_send, share_recv, back_send, back_recv,
    sum_send, sum_recv,
):
    owner = lax.axis_index("kr")
    me = lax.axis_index("kc")
    neighbours = (lax.rem(owner + owners - 1, owners), lax.rem(owner + 1, owners))
    slab = screened.shape[0]
    group_rows = valence.shape[1] // 3
    rows = group_rows // cuts
    pairs = rows // bands
    out_rows = out.shape[1]
    tile = min(256, slab)

    def peer(step):
        return lax.rem(me + step, shares)

    def behind(step):
        return lax.rem(me + shares - step, shares)

    def piece(side, k):
        return (side + 1) * cuts + k

    def go(side, k):
        j = piece(side, k)
        return pltpu.make_async_remote_copy(
            src_ref=valence_hbm.at[at(j, rows)],
            dst_ref=valence.at[me, at(j, rows)],
            send_sem=go_send.at[side, k],
            recv_sem=go_recv.at[side, k],
            device_id={"kr": neighbours[side]},
            device_id_type=pl.DeviceIdType.MESH,
        )

    def share(step, j, source, sender):
        return pltpu.make_async_remote_copy(
            src_ref=source,
            dst_ref=valence.at[sender, at(j, rows)],
            send_sem=share_send.at[step - 1, j],
            recv_sem=share_recv.at[step - 1, j],
            device_id={"kc": peer(step)},
            device_id_type=pl.DeviceIdType.MESH,
        )

    def share_own(step, k):
        return share(step, k, valence_hbm.at[at(k, rows)], me)

    def share_piece(step, j):
        return share(step, j, valence.at[me, at(j, rows)], me)

    def shared(step, j):
        return share(step, j, valence.at[me, at(j, rows)], behind(step))

    def back(side, k):
        j = piece(side, k)
        return pltpu.make_async_remote_copy(
            src_ref=applied.at[at(j, rows)],
            dst_ref=returned.at[at(j - cuts, rows)],
            send_sem=back_send.at[side, k],
            recv_sem=back_recv.at[side, k],
            device_id={"kr": neighbours[1 - side]},
            device_id_type=pl.DeviceIdType.MESH,
        )

    def summand(step, j):
        return pltpu.make_async_remote_copy(
            src_ref=partial.at[at(j, pairs), at(peer(step), out_rows)],
            dst_ref=others.at[step - 1, at(j, pairs)],
            send_sem=sum_send.at[step - 1, j],
            recv_sem=sum_recv.at[step - 1, j],
            device_id={"kc": peer(step)},
            device_id_type=pl.DeviceIdType.MESH,
        )

    def apply(j):
        block = at(j, rows)

        def one(t, carry):
            total = jnp.zeros((rows, tile), jnp.float32)
            for part in range(shares):
                total += lax.dot_general(
                    valence[part, block],
                    screened[at(t, tile), part * slab : (part + 1) * slab],
                    over_last,
                    preferred_element_type=jnp.float32,
                )
            row = me * slab + t * tile + lax.broadcasted_iota(jnp.int32, (rows, tile), 1)
            total = jnp.where(row < sphere, total, 0.0)
            applied[block, at(t, tile)] = total.astype(applied.dtype)
            return carry

        lax.fori_loop(0, slab // tile, one, 0)

    def contract(j, source, k):
        product = lax.dot_general(
            conduction[at(j, rows)], source[at(k, rows)], over_last,
            preferred_element_type=jnp.float32,
        )
        for p in range(pairs):
            band = slice(p * bands, (p + 1) * bands)
            partial[j * pairs + p] = product[band, band]
        for step in range(1, shares):
            summand(step, j).start()

    barrier = pltpu.get_barrier_semaphore()
    for neighbour in neighbours:
        pl.semaphore_signal(
            barrier, inc=1, device_id={"kr": neighbour}, device_id_type=pl.DeviceIdType.MESH
        )
    for step in range(1, shares):
        pl.semaphore_signal(
            barrier, inc=1, device_id={"kc": peer(step)}, device_id_type=pl.DeviceIdType.MESH
        )
    load_screened = pltpu.make_async_copy(screened_hbm, screened, load_sem.at[0])
    load_valence = pltpu.make_async_copy(
        valence_hbm.at[pl.ds(0, group_rows)], valence.at[me, pl.ds(0, group_rows)], load_sem.at[1]
    )
    load_conduction = pltpu.make_async_copy(conduction_hbm, conduction, load_sem.at[2])
    pl.semaphore_wait(barrier, 2 + shares - 1)

    for k in range(cuts):
        for side in range(2):
            go(side, k).start()
    load_screened.start()
    load_valence.start()
    for k in range(cuts):
        for step in range(1, shares):
            share_own(step, k).start()
    load_conduction.start()

    sphere = sizes[owner]
    inside = lax.broadcasted_iota(jnp.int32, (1, screened.shape[1]), 1) < sphere
    keep = jnp.where(inside, 1.0, 0.0).astype(screened.dtype)
    load_screened.wait()
    strip = 64

    def mask(t, carry):
        screened[at(t, strip)] = screened[at(t, strip)] * keep
        return carry

    lax.fori_loop(0, slab // strip, mask, 0)
    load_valence.wait()
    load_conduction.wait()

    def own(k, carry):
        for step in range(1, shares):
            shared(step, k).wait_recv()
        apply(k)
        contract(k, applied, k)
        return carry

    lax.fori_loop(0, cuts, own, 0)

    def finish(k):
        for side in range(2):
            back(side, k).wait()
            contract(piece(side, k), returned, piece(side, k) - cuts)

    def travelling(k, carry):
        for side in range(2):
            go(side, k).wait_recv()
            for step in range(1, shares):
                share_piece(step, piece(side, k)).start()
        for side in range(2):
            j = piece(side, k)
            for step in range(1, shares):
                shared(step, j).wait_recv()
            apply(j)
            back(side, k).start()

        @pl.when(k > 0)
        def _():
            finish(k - 1)

        return carry

    lax.fori_loop(0, cuts, travelling, 0)
    finish(cuts - 1)

    def drain(j, carry):
        for step in range(1, shares):
            share_piece(step, j).wait_send()
            summand(step, j).wait()
        for p in range(pairs):
            pair = j * pairs + p
            total = partial[pair, at(me, out_rows)]
            for step in range(1, shares):
                total += others[step - 1, pair]
            out[pair] = total * prefactor
        return carry

    lax.fori_loop(0, 3 * cuts, drain, 0)
    for k in range(cuts):
        for side in range(2):
            go(side, k).wait_send()


def shards(owners, shares, pair_conduction, pair_valence, screened, sphere_sizes):
    count, bands, slab = pair_valence.shape
    gvectors = screened.shape[2]
    cuts = 4
    out_rows = pair_conduction.shape[1] // shares
    rows = count * bands
    dtype = pair_valence.dtype
    dma = pltpu.SemaphoreType.DMA
    anywhere = pl.BlockSpec(memory_space=pl.ANY)
    return pl.pallas_call(
        functools.partial(kernel, owners, shares, cuts, bands),
        out_shape=jax.ShapeDtypeStruct((count, out_rows, bands), jnp.float32),
        in_specs=[pl.BlockSpec(memory_space=pltpu.SMEM), anywhere, anywhere, anywhere],
        out_specs=pl.BlockSpec(memory_space=pltpu.VMEM),
        scratch_shapes=[
            pltpu.VMEM((slab, gvectors), dtype),
            pltpu.VMEM((rows, slab), dtype),
            pltpu.VMEM((shares, rows, slab), dtype),
            pltpu.VMEM((rows, slab), dtype),
            pltpu.VMEM((rows // 3 * 2, slab), dtype),
            pltpu.VMEM((count, bands, bands), jnp.float32),
            pltpu.VMEM((shares - 1, count, out_rows, bands), jnp.float32),
            dma((3,)),
            dma((2, cuts)),
            dma((2, cuts)),
            dma((shares - 1, 3 * cuts)),
            dma((shares - 1, 3 * cuts)),
            dma((2, cuts)),
            dma((2, cuts)),
            dma((shares - 1, 3 * cuts)),
            dma((shares - 1, 3 * cuts)),
        ],
        compiler_params=pltpu.CompilerParams(
            collective_id=0, has_side_effects=True, vmem_limit_bytes=58 * 1024 * 1024
        ),
        cost_estimate=pl.CostEstimate(
            flops=2 * rows * slab * gvectors + 2 * rows * bands * slab,
            bytes_accessed=2 * (2 * rows * slab + slab * gvectors),
            transcendentals=0,
        ),
    )(
        sphere_sizes,
        pair_conduction.reshape(rows, slab),
        pair_valence.reshape(rows, slab),
        screened.reshape(slab, gvectors),
    )


def solution(mesh):
    return jax.shard_map(
        functools.partial(shards, mesh.shape["kr"], mesh.shape["kc"]),
        mesh=mesh,
        in_specs=(P("kr", None, "kc"), P("kr", None, "kc"), P("kr", "kc", None), P()),
        out_specs=P("kr", "kc", None),
        check_vma=False,
    )
```

```python
import functools

import jax
import jax.numpy as jnp
from jax import lax
from jax.experimental import pallas as pl
from jax.experimental.pallas import tpu as pltpu
from jax.sharding import PartitionSpec as P

prefactor = 0.015625
over_last = (((1,), (1,)), ((), ()))


def at(index, size):
    return pl.ds(pl.multiple_of(index * size, size), size)


def kernel(
    owners, shares, cuts, bands,
    sizes, conduction_hbm, valence_hbm, screened_hbm, out,
    screened, conduction, valence, applied, returned, partial, others,
    load_sem, go_send, go_recv, share_send, share_recv, back_send, back_recv,
    sum_send, sum_recv,
):
    owner = lax.axis_index("kr")
    me = lax.axis_index("kc")
    neighbours = (lax.rem(owner + owners - 1, owners), lax.rem(owner + 1, owners))
    slab = screened.shape[0]
    group_rows = valence.shape[1] // 3
    rows = group_rows // cuts
    pairs = rows // bands
    out_rows = out.shape[1]
    tile = min(256, slab)

    def peer(step):
        return lax.rem(me + step, shares)

    def behind(step):
        return lax.rem(me + shares - step, shares)

    def piece(side, k):
        return (side + 1) * cuts + k

    def go(side, k):
        j = piece(side, k)
        return pltpu.make_async_remote_copy(
            src_ref=valence_hbm.at[at(j, rows)],
            dst_ref=valence.at[me, at(j, rows)],
            send_sem=go_send.at[side, k],
            recv_sem=go_recv.at[side, k],
            device_id={"kr": neighbours[side]},
            device_id_type=pl.DeviceIdType.MESH,
        )

    def share(step, j, source, sender):
        return pltpu.make_async_remote_copy(
            src_ref=source,
            dst_ref=valence.at[sender, at(j, rows)],
            send_sem=share_send.at[step - 1, j],
            recv_sem=share_recv.at[step - 1, j],
            device_id={"kc": peer(step)},
            device_id_type=pl.DeviceIdType.MESH,
        )

    def share_own(step, k):
        return share(step, k, valence_hbm.at[at(k, rows)], me)

    def share_piece(step, j):
        return share(step, j, valence.at[me, at(j, rows)], me)

    def shared(step, j):
        return share(step, j, valence.at[me, at(j, rows)], behind(step))

    def back(side, k):
        j = piece(side, k)
        return pltpu.make_async_remote_copy(
            src_ref=applied.at[at(j, rows)],
            dst_ref=returned.at[at(j - cuts, rows)],
            send_sem=back_send.at[side, k],
            recv_sem=back_recv.at[side, k],
            device_id={"kr": neighbours[1 - side]},
            device_id_type=pl.DeviceIdType.MESH,
        )

    def summand(step, j):
        return pltpu.make_async_remote_copy(
            src_ref=partial.at[at(j, pairs), at(peer(step), out_rows)],
            dst_ref=others.at[step - 1, at(j, pairs)],
            send_sem=sum_send.at[step - 1, j],
            recv_sem=sum_recv.at[step - 1, j],
            device_id={"kc": peer(step)},
            device_id_type=pl.DeviceIdType.MESH,
        )

    def apply(j):
        block = at(j, rows)

        def one(t, carry):
            total = jnp.zeros((rows, tile), jnp.float32)
            for part in range(shares):
                total += lax.dot_general(
                    valence[part, block],
                    screened[at(t, tile), part * slab : (part + 1) * slab],
                    over_last,
                    preferred_element_type=jnp.float32,
                )
            row = me * slab + t * tile + lax.broadcasted_iota(jnp.int32, (rows, tile), 1)
            total = jnp.where(row < sphere, total, 0.0)
            applied[block, at(t, tile)] = total.astype(applied.dtype)
            return carry

        lax.fori_loop(0, slab // tile, one, 0)

    def contract(j, source, k):
        product = lax.dot_general(
            conduction[at(j, rows)], source[at(k, rows)], over_last,
            preferred_element_type=jnp.float32,
        )
        for p in range(pairs):
            band = slice(p * bands, (p + 1) * bands)
            partial[j * pairs + p] = product[band, band]
        for step in range(1, shares):
            summand(step, j).start()

    barrier = pltpu.get_barrier_semaphore()
    for neighbour in neighbours:
        pl.semaphore_signal(
            barrier, inc=1, device_id={"kr": neighbour}, device_id_type=pl.DeviceIdType.MESH
        )
    for step in range(1, shares):
        pl.semaphore_signal(
            barrier, inc=1, device_id={"kc": peer(step)}, device_id_type=pl.DeviceIdType.MESH
        )
    load_screened = pltpu.make_async_copy(screened_hbm, screened, load_sem.at[0])
    load_valence = pltpu.make_async_copy(
        valence_hbm.at[pl.ds(0, group_rows)], valence.at[me, pl.ds(0, group_rows)], load_sem.at[1]
    )
    load_conduction = pltpu.make_async_copy(conduction_hbm, conduction, load_sem.at[2])
    pl.semaphore_wait(barrier, 2 + shares - 1)

    for k in range(cuts):
        for side in range(2):
            go(side, k).start()
    load_screened.start()
    load_valence.start()
    for k in range(cuts):
        for step in range(1, shares):
            share_own(step, k).start()
    load_conduction.start()

    sphere = sizes[owner]
    inside = lax.broadcasted_iota(jnp.int32, (1, screened.shape[1]), 1) < sphere
    keep = jnp.where(inside, 1.0, 0.0).astype(screened.dtype)
    load_screened.wait()
    strip = 64

    def mask(t, carry):
        screened[at(t, strip)] = screened[at(t, strip)] * keep
        return carry

    lax.fori_loop(0, slab // strip, mask, 0)
    load_valence.wait()
    load_conduction.wait()

    def own(k, carry):
        for step in range(1, shares):
            shared(step, k).wait_recv()
        apply(k)
        contract(k, applied, k)
        return carry

    lax.fori_loop(0, cuts, own, 0)

    def travelling(k, carry):
        for side in range(2):
            go(side, k).wait_recv()
            for step in range(1, shares):
                share_piece(step, piece(side, k)).start()
        for side in range(2):
            j = piece(side, k)
            for step in range(1, shares):
                shared(step, j).wait_recv()
            apply(j)
            back(side, k).start()
        return carry

    lax.fori_loop(0, cuts, travelling, 0)

    def drain(j, carry):
        for step in range(1, shares):
            share_piece(step, j).wait_send()
            summand(step, j).wait()
        for p in range(pairs):
            pair = j * pairs + p
            total = partial[pair, at(me, out_rows)]
            for step in range(1, shares):
                total += others[step - 1, pair]
            out[pair] = total
        return carry

    lax.fori_loop(0, cuts, drain, 0)
    for k in range(cuts):
        for side in range(2):
            go(side, k).wait_send()

    def finish(k, carry):
        for side in range(2):
            j = piece(side, k)
            back(side, k).wait()
            contract(j, returned, j - cuts)

        @pl.when(k > 0)
        def _():
            for side in range(2):
                drain(piece(side, k - 1), carry)

        return carry

    lax.fori_loop(0, cuts, finish, 0)
    for side in range(2):
        drain(piece(side, cuts - 1), 0)


def shards(owners, shares, pair_conduction, pair_valence, screened, sphere_sizes):
    count, bands, slab = pair_valence.shape
    gvectors = screened.shape[2]
    cuts = count // 3
    out_rows = pair_conduction.shape[1] // shares
    rows = count * bands
    dtype = pair_valence.dtype
    dma = pltpu.SemaphoreType.DMA
    anywhere = pl.BlockSpec(memory_space=pl.ANY)
    summed = pl.pallas_call(
        functools.partial(kernel, owners, shares, cuts, bands),
        out_shape=jax.ShapeDtypeStruct((count, out_rows, bands), jnp.float32),
        in_specs=[pl.BlockSpec(memory_space=pltpu.SMEM), anywhere, anywhere, anywhere],
        out_specs=pl.BlockSpec(memory_space=pltpu.VMEM),
        scratch_shapes=[
            pltpu.VMEM((slab, gvectors), dtype),
            pltpu.VMEM((rows, slab), dtype),
            pltpu.VMEM((shares, rows, slab), dtype),
            pltpu.VMEM((rows, slab), dtype),
            pltpu.VMEM((rows // 3 * 2, slab), dtype),
            pltpu.VMEM((count, bands, bands), jnp.float32),
            pltpu.VMEM((shares - 1, count, out_rows, bands), jnp.float32),
            dma((3,)),
            dma((2, cuts)),
            dma((2, cuts)),
            dma((shares - 1, 3 * cuts)),
            dma((shares - 1, 3 * cuts)),
            dma((2, cuts)),
            dma((2, cuts)),
            dma((shares - 1, 3 * cuts)),
            dma((shares - 1, 3 * cuts)),
        ],
        compiler_params=pltpu.CompilerParams(
            collective_id=0, has_side_effects=True, vmem_limit_bytes=50 * 1024 * 1024
        ),
        cost_estimate=pl.CostEstimate(
            flops=2 * rows * slab * gvectors + 2 * rows * bands * slab,
            bytes_accessed=2 * (2 * rows * slab + slab * gvectors),
            transcendentals=0,
        ),
    )(
        sphere_sizes,
        pair_conduction.reshape(rows, slab),
        pair_valence.reshape(rows, slab),
        screened.reshape(slab, gvectors),
    )
    return summed * prefactor


def solution(mesh):
    return jax.shard_map(
        functools.partial(shards, mesh.shape["kr"], mesh.shape["kc"]),
        mesh=mesh,
        in_specs=(P("kr", None, "kc"), P("kr", None, "kc"), P("kr", "kc", None), P()),
        out_specs=P("kr", "kc", None),
        check_vma=False,
    )
```
